32 devices in a mesh: ta: 8 (over z, core), gz: 4 (over y, x).
Axes of the slice: x: 2, y: 2, z: 4, core: 2. Of those that a mesh axis runs over, the one named last changes fastest.
Arguments:
- source: bfloat16 [2, 4, 3, 8, 16, 512], P(None, None, None, 'ta', 'gz'), may hold values from -6 to 6
- gauge_links: bfloat16 [4, 2, 3, 3, 8, 16, 512], P(None, None, None, None, 'ta', 'gz'), may hold values from -2.5 to 2.5
- clover_diag: float32 [4, 3, 8, 16, 512], P(None, None, 'ta', 'gz'), may hold values from 0.5 to 4
- agg_map: int32 [8, 16, 512], P('ta', 'gz'), may hold values from 0 to 31
- prolong: bfloat16 [24, 2, 4, 3, 8, 16, 512], P(None, None, None, None, 'ta', 'gz'), may hold values from -0.078125 to 0.078125
- coarse_inverse: float32 [8, 768, 768], P('ta', 'gz'), may hold values from -16 to 16
Outputs:
- solution: float32 [2, 4, 3, 8, 16, 512], P(None, None, None, 'ta', 'gz')
The draws below stay inside these ranges and needn't reach their ends.
Inputs may be any that keep to these rules, and one draw needn't show every extreme that they name: `agg_map`: aggregate numbers are local to each group of 4 devices along gz.
All inputs are finite; a program needn't handle non-finite values.
Results may differ from the reference program's by a relative error of at most 0.03.
Values may be sent and summed in bfloat16 or wider, within the bound.
A program may use at most 64 MiB of HBM per device.

```python
import math
import jax
import jax.numpy as jnp
from jax import lax

LX = 32
LY = 16
TL = 1
NV = 24
NAGG = 32
SITES = 512
T_ALL = 8
Z_ALL = 16
NC = 768
AGG_SITES = 256
N_TA = 8


def place_ends(values, key, smallest, largest):
    index_at = [jax.random.randint(jax.random.fold_in(key, axis), (), 0, length) for axis, length in enumerate(values.shape)]
    widest = values.shape.index(max(values.shape))
    beside = index_at[:widest] + [(index_at[widest] + 1) % values.shape[widest]] + index_at[widest + 1:]
    return values.at[tuple(index_at)].set(smallest).at[tuple(beside)].set(largest)


def block_scale(own_key, shape, shards, least, largest):
    def one(axis_at, blocks):
        steps = jax.random.uniform(jax.random.fold_in(jax.random.fold_in(own_key, 6), axis_at), (blocks,), jnp.float32, least / len(shards), largest / len(shards))
        return jnp.repeat(jnp.exp(steps), shape[axis_at] // blocks).reshape((-1,) + (1,) * (len(shape) - axis_at - 1))

    level = one(*shards[0])
    for cut in shards[1:]:
        level = level * one(*cut)
    return level


def noise(rng, shape, scale, limit, shards=(), kind=jnp.bfloat16):
    array = scale * jax.random.normal(rng, shape, jnp.float32)
    if shards:
        array = array * block_scale(rng, shape, shards, -0.22, 0.18)
    return jnp.clip(array, -limit, limit).astype(kind)


def setup_inputs(seed: int = 0) -> dict:
    arg_keys = jax.random.split(jax.random.key(seed), 7)
    return {
        "source": noise(arg_keys[0], (2, 4, 3, T_ALL, Z_ALL, SITES), 1.0, 6.0, ((3, 8), (4, 4))),
        "gauge_links": noise(arg_keys[1], (4, 2, 3, 3, T_ALL, Z_ALL, SITES), 6 ** -0.5, 2.5, ((4, 8), (5, 4))),
        "clover_diag": jnp.clip(jnp.exp(math.log(4.0) - 2.0794415 * jax.random.uniform(arg_keys[2], (4, 3, T_ALL, Z_ALL, SITES), jnp.float32) ** block_scale(arg_keys[2], (4, 3, T_ALL, Z_ALL, SITES), ((2, 8), (3, 4)), -0.2, 0.2)), 0.5, 4.0),
        "agg_map": place_ends(jax.random.randint(arg_keys[3], (T_ALL, Z_ALL, SITES), 0, NAGG), jax.random.fold_in(arg_keys[3], 1), 0, NAGG - 1).astype(jnp.int32),
        "prolong": noise(arg_keys[4], (NV, 2, 4, 3, T_ALL, Z_ALL, SITES), (24 * AGG_SITES) ** -0.5, 0.078125, ((4, 8), (5, 4))),
        "coarse_inverse": noise(arg_keys[5], (N_TA, NC, NC), (3 * (AGG_SITES // NC + 1) ** 0.5), 16.0, ((0, 8), (1, 4)), jnp.float32),
    }


mass_shift = -0.4
spin_perms = ((3, 2, 1, 0), (3, 2, 1, 0), (2, 3, 0, 1), (2, 3, 0, 1))
spin_real = ((0.0, 0.0, 0.0, 0.0), (-1.0, 1.0, 1.0, -1.0), (0.0, 0.0, 0.0, 0.0), (1.0, 1.0, 1.0, 1.0))
spin_imag = ((-1.0, -1.0, 1.0, 1.0), (0.0, 0.0, 0.0, 0.0), (-1.0, 1.0, 1.0, -1.0), (0.0, 0.0, 0.0, 0.0))


def phase_mul(coef_re, coef_im, value_re, value_im):
    if coef_im == 0.0:
        return coef_re * value_re, coef_re * value_im
    return -coef_im * value_im, coef_im * value_re


def project(wide, direction, sign):
    rows_re = []
    rows_im = []
    for slot in range(2):
        other = spin_perms[direction][slot]
        term_re, term_im = phase_mul(spin_real[direction][slot], spin_imag[direction][slot], wide[0, other], wide[1, other])
        rows_re.append(wide[0, slot] + sign * term_re)
        rows_im.append(wide[1, slot] + sign * term_im)
    return jnp.stack([jnp.stack(rows_re), jnp.stack(rows_im)])


def expand(half, direction, sign):
    rows_re = [None] * 4
    rows_im = [None] * 4
    for slot in range(2):
        other = spin_perms[direction][slot]
        rows_re[slot] = half[0, slot]
        rows_im[slot] = half[1, slot]
        term_re, term_im = phase_mul(spin_real[direction][other], spin_imag[direction][other], half[0, slot], half[1, slot])
        rows_re[other] = sign * term_re
        rows_im[other] = sign * term_im
    return jnp.stack([jnp.stack(rows_re), jnp.stack(rows_im)])


def color_mix(link_pair, spinor, dagger):
    link_re = link_pair[0].astype(jnp.float32)
    link_im = link_pair[1].astype(jnp.float32)
    spin_re = spinor[0].astype(jnp.float32)
    spin_im = spinor[1].astype(jnp.float32)
    out_re = []
    out_im = []
    for row in range(3):
        acc_re = None
        acc_im = None
        for col in range(3):
            if dagger:
                entry_re = link_re[col, row]
                entry_im = -link_im[col, row]
            else:
                entry_re = link_re[row, col]
                entry_im = link_im[row, col]
            part_re = entry_re * spin_re[:, col] - entry_im * spin_im[:, col]
            part_im = entry_re * spin_im[:, col] + entry_im * spin_re[:, col]
            acc_re = part_re if acc_re is None else acc_re + part_re
            acc_im = part_im if acc_im is None else acc_im + part_im
        out_re.append(acc_re)
        out_im.append(acc_im)
    return jnp.stack([jnp.stack(out_re, axis=1), jnp.stack(out_im, axis=1)])


def neighbour(values, direction, step):
    if direction == 3:
        return jnp.roll(values, -step, axis=-3)
    if direction == 2:
        return jnp.roll(values, -step, axis=-2)
    dims_all = values.shape
    grid = values.reshape(dims_all[:-1] + (LY, LX))
    rolled = jnp.roll(grid, -step, axis=-1 if direction == 0 else -2)
    return rolled.reshape(dims_all)


def hopping(spinor, gauge_links):
    wide = spinor.astype(jnp.float32)
    total = jnp.zeros(spinor.shape, jnp.float32)
    for direction in range(4):
        fwd_half = lax.optimization_barrier(project(wide, direction, -1.0).astype(jnp.bfloat16))
        ahead = neighbour(fwd_half, direction, 1)
        total = total + expand(color_mix(gauge_links[direction], ahead, False), direction, -1.0)
        back_half = lax.optimization_barrier(project(color_mix(gauge_links[direction], spinor, True), direction, 1.0).astype(jnp.bfloat16))
        behind = neighbour(back_half, direction, -1).astype(jnp.float32)
        total = total + expand(behind, direction, 1.0)
    return total


def reference(source, gauge_links, clover_diag, agg_map, prolong, coarse_inverse):
    hp = lax.Precision.HIGHEST
    diagonal = 4.0 + mass_shift + clover_diag
    source_wide = source.astype(jnp.float32)
    first_iter = source_wide / diagonal
    first_half = first_iter.astype(jnp.bfloat16)
    first_resid = source_wide - diagonal * first_iter + 0.5 * hopping(first_half, gauge_links)
    second_iter = first_iter + first_resid / diagonal
    second_half = second_iter.astype(jnp.bfloat16)
    second_resid = source_wide - diagonal * second_iter + 0.5 * hopping(second_half, gauge_links)
    resid_half = second_resid.astype(jnp.bfloat16)
    labels = jnp.arange(NAGG, dtype=jnp.int32)

    def restrict_slice(slice_index):
        prolong_slice = lax.dynamic_index_in_dim(prolong, slice_index, 4, keepdims=False).astype(jnp.float32)
        resid_slice = lax.dynamic_index_in_dim(resid_half, slice_index, 3, keepdims=False).astype(jnp.float32)
        map_slice = lax.dynamic_index_in_dim(agg_map, slice_index, 0, keepdims=False)
        projected = jnp.einsum("vrsczn,rsczn->vzn", prolong_slice, resid_slice, precision=hp)
        member = (map_slice.reshape(-1)[None, :] == labels[:, None]).astype(jnp.float32)
        return jnp.einsum("am,vm->av", member, projected.reshape(NV, -1), precision=hp)

    partial_all = lax.map(restrict_slice, jnp.arange(T_ALL, dtype=jnp.int32))
    coarse_resid = partial_all.reshape(N_TA, TL, NC).sum(axis=1)
    correction = jnp.einsum("gij,gj->gi", coarse_inverse, coarse_resid, precision=hp)
    correction_half = correction.astype(jnp.bfloat16)

    def prolong_slice_fn(slice_index):
        group_index = slice_index // TL
        prolong_slice = lax.dynamic_index_in_dim(prolong, slice_index, 4, keepdims=False).astype(jnp.float32)
        map_slice = lax.dynamic_index_in_dim(agg_map, slice_index, 0, keepdims=False)
        values_here = lax.dynamic_index_in_dim(correction_half, group_index, 0, keepdims=False).astype(jnp.float32).reshape(NAGG, NV)
        member = (map_slice.reshape(-1)[None, :] == labels[:, None]).astype(jnp.float32)
        spread = jnp.einsum("av,am->vm", values_here, member, precision=hp).reshape(NV, Z_ALL, SITES)
        return jnp.einsum("vrsczn,vzn->rsczn", prolong_slice, spread, precision=hp)

    smooth = lax.map(prolong_slice_fn, jnp.arange(T_ALL, dtype=jnp.int32))
    return second_iter + jnp.moveaxis(smooth, 0, 3)
```

```python
import functools

import jax
import jax.numpy as jnp
from jax import lax
from jax.experimental import pallas as pl
from jax.experimental.pallas import tpu as pltpu
from jax.sharding import PartitionSpec as P

LX = 32
NAGG = 32
NV = 24
NCOMP = 24
HALF = 256
GROUPS = 8

MESH = pl.DeviceIdType.MESH
F32 = jnp.float32
BF16 = jnp.bfloat16

spin_perms = ((3, 2, 1, 0), (3, 2, 1, 0), (2, 3, 0, 1), (2, 3, 0, 1))
spin_coefs = (
    ((1, -1), (1, -1), (1, 1), (1, 1)),
    ((0, -1), (0, 1), (0, 1), (0, -1)),
    ((1, -1), (1, 1), (1, 1), (1, -1)),
    ((0, 1), (0, 1), (0, 1), (0, 1)),
)


def add_signed(base, sign, value):
    return base + value if sign > 0 else base - value


def phase_terms(coef, sign):
    imag, coef_sign = coef
    total_sign = coef_sign * sign
    if imag:
        return (1, -total_sign), (0, total_sign)
    return (0, total_sign), (1, total_sign)


def project(field, direction, sign):
    parts = [[None, None], [None, None]]
    for slot in range(2):
        other = spin_perms[direction][slot]
        terms = phase_terms(spin_coefs[direction][slot], sign)
        for part in range(2):
            from_part, term_sign = terms[part]
            parts[part][slot] = add_signed(
                field[pl.ds(part * 12 + slot * 3, 3)],
                term_sign,
                field[pl.ds(from_part * 12 + other * 3, 3)],
            )
    return parts


def accumulate(total, half, direction, sign):
    for slot in range(2):
        other = spin_perms[direction][slot]
        terms = phase_terms(spin_coefs[direction][other], sign)
        for part in range(2):
            at = pl.ds(part * 12 + slot * 3, 3)
            total[at] = total[at] + half[part][slot]
            from_part, term_sign = terms[part]
            at = pl.ds(part * 12 + other * 3, 3)
            total[at] = add_signed(total[at], term_sign, half[from_part][slot])


def mix(links, direction, half, dagger):
    out = [[None, None], [None, None]]
    for slot in range(2):
        acc_re = acc_im = None
        for col in range(3):
            if dagger:
                link_re = links[direction, 0, col]
                link_im = links[direction, 1, col]
            else:
                link_re = links[direction, 0, :, col]
                link_im = links[direction, 1, :, col]
            re = half[0][slot][col][None]
            im = half[1][slot][col][None]
            if dagger:
                part_re = link_re * re + link_im * im
                part_im = link_re * im - link_im * re
            else:
                part_re = link_re * re - link_im * im
                part_im = link_re * im + link_im * re
            acc_re = part_re if acc_re is None else acc_re + part_re
            acc_im = part_im if acc_im is None else acc_im + part_im
        out[0][slot] = acc_re
        out[1][slot] = acc_im
    return out


def per_part(fn, half):
    return [[fn(half[part][slot]) for slot in range(2)] for part in range(2)]


def stack_half(half):
    return jnp.concatenate([half[p][s] for p in range(2) for s in range(2)], axis=0)


def split_half(stacked):
    return [[stacked[p * 6 + s * 3 : p * 6 + s * 3 + 3] for s in range(2)] for p in range(2)]


def split_bf16(value, pieces):
    out = []
    for _ in range(pieces):
        piece = value.astype(BF16)
        out.append(piece)
        value = value - piece.astype(F32)
    return out


def kernel(
    n_ta,
    n_gz,
    rows,
    source_hbm,
    links_hbm,
    clover_hbm,
    map_hbm,
    prolong_hbm,
    inverse_hbm,
    out_ref,
    source_in,
    links_in,
    clover_in,
    map_in,
    prolong_in,
    inverse,
    source,
    links,
    diag,
    recip,
    prolong,
    field,
    total,
    member,
    expander,
    projected,
    t_send,
    t_recv,
    z_send,
    z_recv,
    r_send,
    r_recv,
    c_send,
    c_recv,
    in_sem,
    halo_send_sem,
    halo_recv_sem,
    r_send_sem,
    r_recv_sem,
    c_send_sem,
    c_recv_sem,
):
    loads = [
        pltpu.make_async_copy(src, dst, in_sem.at[i])
        for i, (src, dst) in enumerate(
            (
                (source_hbm, source_in),
                (clover_hbm, clover_in),
                (links_hbm, links_in),
                (map_hbm, map_in),
                (prolong_hbm, prolong_in),
                (inverse_hbm, inverse),
            )
        )
    ]
    for load in loads:
        load.start()
    load_source, load_clover, load_links, load_map, load_prolong, load_inverse = loads

    ta = lax.axis_index("ta")
    gz = lax.axis_index("gz")
    t_before = lax.rem(ta + n_ta - 1, n_ta)
    t_after = lax.rem(ta + 1, n_ta)
    z_before = lax.rem(gz + n_gz - 1, n_gz)
    z_after = lax.rem(gz + 1, n_gz)
    peers = [lax.rem(gz + k, n_gz) for k in range(1, n_gz)]

    barrier = pltpu.get_barrier_semaphore()
    for there in (t_before, t_after):
        pl.semaphore_signal(barrier, inc=1, device_id=(there, gz), device_id_type=MESH)
    for there in peers:
        pl.semaphore_signal(barrier, inc=1, device_id=(ta, there), device_id_type=MESH)

    sub = lax.broadcasted_iota(jnp.int32, (8, HALF), 0)
    lane = lax.broadcasted_iota(jnp.int32, (8, HALF), 1)
    z_at = jnp.bitwise_and(sub, 3)
    x_at = jnp.bitwise_and(lane, LX - 1)

    def widen(dst, src, at, size):
        block = src[pl.ds(at, size)].astype(F32)
        dst[pl.ds(at, size), 0:4, :] = block[:, :, :HALF]
        dst[pl.ds(at, size), 4:8, :] = block[:, :, HALF:]

    load_source.wait()
    widen(source, source_in, 0, NCOMP)
    load_clover.wait()
    widen(diag, clover_in, 0, 12)
    for at in range(0, 12, 3):
        here = pl.ds(at, 3)
        wide = diag[here] + 3.6
        diag[here] = wide
        inv = 1.0 / wide
        recip[here] = inv
        for part in range(2):
            there = pl.ds(part * 12 + at, 3)
            field[there] = source[there] * inv

    pl.semaphore_wait(barrier, 2 + n_gz - 1)

    def select(mask, first, second):
        return jnp.where(mask[None], first, second)

    def shift(direction, step):
        def x_shift(value):
            if step > 0:
                return select(
                    x_at == LX - 1, pltpu.roll(value, LX - 1, 2), pltpu.roll(value, HALF - 1, 2)
                )
            return select(x_at == 0, pltpu.roll(value, HALF - LX + 1, 2), pltpu.roll(value, 1, 2))

        def y_shift(value):
            rolled = pltpu.roll(value, HALF - LX if step > 0 else LX, 2)
            swapped = pltpu.roll(rolled, 4, 1)
            return select(lane >= HALF - LX if step > 0 else lane < LX, swapped, rolled)

        return x_shift if direction == 0 else y_shift

    def pack_rows(stacked, row):
        blocks = []
        for block in range(3):
            packed = None
            for j in range(4):
                value = stacked[block * 4 + j]
                turn = (j - row) % 8
                if turn:
                    value = pltpu.roll(value, turn, 0)
                packed = value if packed is None else jnp.where(z_at == j, value, packed)
            blocks.append(packed)
        blocks.append(jnp.zeros((8, HALF), F32))
        return jnp.concatenate(blocks, axis=0).astype(BF16)

    def fill_rows(stacked, packed, row, turn):
        out = []
        for j in range(12):
            halo = packed[j // 4]
            by = (row - j % 4) % 8
            if by:
                halo = pltpu.roll(halo, by, 0)
            out.append(jnp.where(z_at == row, halo, pltpu.roll(stacked[j], turn, 0))[None])
        return jnp.concatenate(out, axis=0)

    def halo_copy(sweep, which, src, dst, device):
        return pltpu.make_async_remote_copy(
            src_ref=src,
            dst_ref=dst,
            send_sem=halo_send_sem.at[sweep, which],
            recv_sem=halo_recv_sem.at[sweep, which],
            device_id=device,
            device_id_type=MESH,
        )

    def hopping(sweep, before_links, beside):
        copies = [
            halo_copy(sweep, 0, t_send.at[sweep, 0], t_recv.at[sweep, 0], (t_before, gz)),
            halo_copy(sweep, 1, t_send.at[sweep, 1], t_recv.at[sweep, 1], (t_after, gz)),
            halo_copy(sweep, 2, z_send.at[sweep, 0], z_recv.at[sweep, 0], (ta, z_before)),
            halo_copy(sweep, 3, z_send.at[sweep, 1], z_recv.at[sweep, 1], (ta, z_after)),
        ]
        fwd_t = stack_half(project(field, 3, -1))
        t_send[sweep, 0] = fwd_t.reshape(96, HALF).astype(BF16)
        copies[0].start()
        fwd_z = stack_half(project(field, 2, -1))
        z_send[sweep, 0] = pack_rows(fwd_z, 0)
        copies[2].start()
        before_links()
        back_t = stack_half(mix(links, 3, project(field, 3, 1), True))
        t_send[sweep, 1] = back_t.reshape(96, HALF).astype(BF16)
        copies[1].start()
        back_z = stack_half(mix(links, 2, project(field, 2, 1), True))
        z_send[sweep, 1] = pack_rows(back_z, 3)
        copies[3].start()

        total[...] = jnp.zeros((NCOMP, 8, HALF), F32)
        for direction in range(2):
            ahead = per_part(shift(direction, 1), project(field, direction, -1))
            accumulate(total, mix(links, direction, ahead, False), direction, -1)
            behind = per_part(
                shift(direction, -1), mix(links, direction, project(field, direction, 1), True)
            )
            accumulate(total, behind, direction, 1)
        beside()
        for copy in copies:
            copy.wait()
        ahead_z = fill_rows(
            stack_half(project(field, 2, -1)),
            z_recv[sweep, 0].astype(F32).reshape(4, 8, HALF),
            3,
            7,
        )
        accumulate(total, mix(links, 2, split_half(ahead_z), False), 2, -1)
        behind_z = fill_rows(back_z, z_recv[sweep, 1].astype(F32).reshape(4, 8, HALF), 0, 1)
        accumulate(total, split_half(behind_z), 2, 1)
        ahead_t = t_recv[sweep, 0].astype(F32).reshape(12, 8, HALF)
        accumulate(total, mix(links, 3, split_half(ahead_t), False), 3, -1)
        behind_t = t_recv[sweep, 1].astype(F32).reshape(12, 8, HALF)
        accumulate(total, split_half(behind_t), 3, 1)

    def widen_links():
        load_links.wait()
        for direction in (3, 2, 1, 0):
            for part in range(2):
                for row in range(3):
                    at = direction * 18 + part * 9 + row * 3
                    block = links_in[pl.ds(at, 3)].astype(F32)
                    links[direction, part, row, :, 0:4, :] = block[:, :, :HALF]
                    links[direction, part, row, :, 4:8, :] = block[:, :, HALF:]

    def widen_prolong(start, stop):
        def step(i, carry):
            widen(prolong, prolong_in, i * 12, 12)
            return carry

        lax.fori_loop(start, stop, step, 0)

    def beside_first():
        load_map.wait()
        labels = lax.broadcasted_iota(jnp.int32, (NAGG, HALF), 0)
        ones = []
        for half in range(2):
            for z in range(4):
                row = map_in[pl.ds(z, 1), pl.ds(half * HALF, HALF)]
                ones.append((labels == row).astype(F32))
        member[...] = jnp.concatenate(ones, axis=0).astype(BF16)
        low = jnp.bitwise_and(
            lax.broadcasted_iota(jnp.int32, (HALF, NV * NAGG), 0), NAGG - 1
        ) * NV
        column = lax.broadcasted_iota(jnp.int32, (HALF, NV * NAGG), 1)
        inside = jnp.logical_and(column >= low, column < low + NV)
        expander[...] = inside.astype(F32).astype(BF16)
        load_prolong.wait()
        widen_prolong(0, 24)

    hopping(0, widen_links, beside_first)
    for at in range(0, 24, 3):
        here = pl.ds(at, 3)
        scale = pl.ds(at % 12, 3)
        first = field[here]
        resid = source[here] - diag[scale] * first + 0.5 * total[here]
        field[here] = first + resid * recip[scale]
    hopping(1, lambda: None, lambda: widen_prolong(24, 48))
    for at in range(0, 24, 3):
        here = pl.ds(at, 3)
        second = field[here]
        total[here] = source[here] - diag[pl.ds(at % 12, 3)] * second + 0.5 * total[here]

    def restrict(i, carry):
        accs = [None] * 4
        for comp in range(NCOMP):
            resid = total[comp]
            for k in range(4):
                term = prolong[(i * 4 + k) * NCOMP + comp] * resid
                accs[k] = term if accs[k] is None else accs[k] + term
        for k in range(4):
            projected[pl.ds((i * 4 + k) * 8, 8)] = accs[k]
        return carry

    lax.fori_loop(0, NV // 4, restrict, 0)

    member_value = member[...]
    sums = None
    for piece in split_bf16(projected[...], 3):
        term = lax.dot_general(
            piece, member_value, (((1,), (1,)), ((), ())), preferred_element_type=F32
        )
        sums = term if sums is None else sums + term
    own_group = (jnp.right_shift(lane, 5) == sub)[None]
    sums = jnp.sum(jnp.where(own_group, sums.reshape(NV, 8, HALF), 0.0), axis=1)
    spread_out = None
    expander_value = expander[...]
    for piece in split_bf16(sums, 3):
        term = jnp.dot(piece, expander_value, preferred_element_type=F32)
        spread_out = term if spread_out is None else spread_out + term
    column = lax.broadcasted_iota(jnp.int32, (NV, NV * NAGG), 1)
    vector = column - NV * jnp.right_shift(column * 2731, 16)
    at_vector = lax.broadcasted_iota(jnp.int32, (NV, NV * NAGG), 0) == vector
    r_send[...] = jnp.sum(jnp.where(at_vector, spread_out, 0.0), axis=0, keepdims=True)

    def to_peers(src, dst, send_sem, recv_sem):
        copies = [
            pltpu.make_async_remote_copy(
                src_ref=src,
                dst_ref=dst.at[k],
                send_sem=send_sem.at[k],
                recv_sem=recv_sem.at[k],
                device_id=(ta, there),
                device_id_type=MESH,
            )
            for k, there in enumerate(peers)
        ]
        for copy in copies:
            copy.start()
        return copies

    copies = to_peers(r_send, r_recv, r_send_sem, r_recv_sem)
    load_inverse.wait()
    for copy in copies:
        copy.wait()
    coarse = r_send[...]
    for k in range(n_gz - 1):
        coarse = coarse + r_recv[k]
    own_rows = jnp.sum(inverse[...] * coarse, axis=1, keepdims=True)
    label = jnp.bitwise_and(lax.broadcasted_iota(jnp.int32, (NV, 128), 1), NAGG - 1)
    owned = rows // NV
    placed = jnp.zeros((NV, 128), F32)
    for k in range(owned):
        placed = jnp.where(label == gz * owned + k, own_rows[k * NV : (k + 1) * NV], placed)
    c_send[...] = placed
    copies = to_peers(c_send, c_recv, c_send_sem, c_recv_sem)
    for copy in copies:
        copy.wait()
    correction = c_send[...]
    for k in range(n_gz - 1):
        correction = correction + c_recv[k]
    correction = jnp.concatenate([correction, correction], axis=1)
    lhs = jnp.where(own_group, jnp.broadcast_to(correction[:, None], (NV, 8, HALF)), 0.0)
    projected[...] = jnp.dot(
        lhs.reshape(NV * 8, HALF).astype(BF16), member_value, preferred_element_type=F32
    )

    def smooth(i, carry):
        accs = [field[i * 4 + k] for k in range(4)]
        for v in range(NV):
            weight = projected[pl.ds(v * 8, 8)]
            for k in range(4):
                accs[k] = accs[k] + prolong[v * NCOMP + i * 4 + k] * weight
        for k in range(4):
            out_ref[i * 4 + k, :, 0:HALF] = accs[k][0:4]
            out_ref[i * 4 + k, :, HALF : 2 * HALF] = accs[k][4:8]
        return carry

    lax.fori_loop(0, NCOMP // 4, smooth, 0)


def shards(n_ta, n_gz, source, links, clover, agg_map, prolong, inverse):
    rows = inverse.shape[1]
    vmem = pltpu.VMEM
    dma = pltpu.SemaphoreType.DMA
    out = pl.pallas_call(
        functools.partial(kernel, n_ta, n_gz, rows),
        out_shape=jax.ShapeDtypeStruct((24, 4, 512), F32),
        in_specs=[pl.BlockSpec(memory_space=pl.ANY)] * 6,
        out_specs=pl.BlockSpec(memory_space=pltpu.VMEM),
        scratch_shapes=[
            vmem((24, 4, 512), BF16),
            vmem((72, 4, 512), BF16),
            vmem((12, 4, 512), F32),
            vmem((4, 512), jnp.int32),
            vmem((576, 4, 512), BF16),
            vmem((rows, 768), F32),
            vmem((24, 8, HALF), F32),
            vmem((4, 2, 3, 3, 8, HALF), F32),
            vmem((12, 8, HALF), F32),
            vmem((12, 8, HALF), F32),
            vmem((576, 8, HALF), F32),
            vmem((24, 8, HALF), F32),
            vmem((24, 8, HALF), F32),
            vmem((256, HALF), BF16),
            vmem((256, 768), BF16),
            vmem((192, HALF), F32),
            vmem((2, 2, 96, HALF), BF16),
            vmem((2, 2, 96, HALF), BF16),
            vmem((2, 2, 32, HALF), BF16),
            vmem((2, 2, 32, HALF), BF16),
            vmem((1, 768), F32),
            vmem((n_gz - 1, 1, 768), F32),
            vmem((NV, 128), F32),
            vmem((n_gz - 1, NV, 128), F32),
            dma((6,)),
            dma((2, 4)),
            dma((2, 4)),
            dma((n_gz - 1,)),
            dma((n_gz - 1,)),
            dma((n_gz - 1,)),
            dma((n_gz - 1,)),
        ],
        compiler_params=pltpu.CompilerParams(
            collective_id=0, has_side_effects=True, vmem_limit_bytes=32 * 1024 * 1024
        ),
        cost_estimate=pl.CostEstimate(flops=20000000, bytes_accessed=4000000, transcendentals=0),
    )(
        source.reshape(24, 4, 512),
        links.reshape(72, 4, 512),
        clover.reshape(12, 4, 512),
        agg_map.reshape(4, 512),
        prolong.reshape(576, 4, 512),
        inverse.reshape(rows, 768),
    )
    return out.reshape(2, 4, 3, 1, 4, 512)


def solution(mesh):
    return jax.shard_map(
        functools.partial(shards, mesh.shape["ta"], mesh.shape["gz"]),
        mesh=mesh,
        in_specs=(
            P(None, None, None, "ta", "gz", None),
            P(None, None, None, None, "ta", "gz", None),
            P(None, None, "ta", "gz", None),
            P("ta", "gz", None),
            P(None, None, None, None, "ta", "gz", None),
            P("ta", "gz", None),
        ),
        out_specs=P(None, None, None, "ta", "gz", None),
        check_vma=False,
    )
```

```python
import functools

import jax
import jax.numpy as jnp
from jax import lax
from jax.experimental import pallas as pl
from jax.experimental.pallas import tpu as pltpu
from jax.sharding import PartitionSpec as P

LX = 32
NAGG = 32
NV = 24
NCOMP = 24
HALF = 256
GROUPS = 8

MESH = pl.DeviceIdType.MESH
F32 = jnp.float32
BF16 = jnp.bfloat16

spin_perms = ((3, 2, 1, 0), (3, 2, 1, 0), (2, 3, 0, 1), (2, 3, 0, 1))
spin_coefs = (
    ((1, -1), (1, -1), (1, 1), (1, 1)),
    ((0, -1), (0, 1), (0, 1), (0, -1)),
    ((1, -1), (1, 1), (1, 1), (1, -1)),
    ((0, 1), (0, 1), (0, 1), (0, 1)),
)


def add_signed(base, sign, value):
    return base + value if sign > 0 else base - value


def phase_terms(coef, sign):
    imag, coef_sign = coef
    total_sign = coef_sign * sign
    if imag:
        return (1, -total_sign), (0, total_sign)
    return (0, total_sign), (1, total_sign)


def project(field, direction, sign):
    parts = [[None, None], [None, None]]
    for slot in range(2):
        other = spin_perms[direction][slot]
        terms = phase_terms(spin_coefs[direction][slot], sign)
        for part in range(2):
            from_part, term_sign = terms[part]
            parts[part][slot] = add_signed(
                field[pl.ds(part * 12 + slot * 3, 3)],
                term_sign,
                field[pl.ds(from_part * 12 + other * 3, 3)],
            )
    return parts


def accumulate(total, half, direction, sign):
    for slot in range(2):
        other = spin_perms[direction][slot]
        terms = phase_terms(spin_coefs[direction][other], sign)
        for part in range(2):
            at = pl.ds(part * 12 + slot * 3, 3)
            total[at] = total[at] + half[part][slot]
            from_part, term_sign = terms[part]
            at = pl.ds(part * 12 + other * 3, 3)
            total[at] = add_signed(total[at], term_sign, half[from_part][slot])


def mix(links, direction, half, dagger):
    out = [[None, None], [None, None]]
    for slot in range(2):
        acc_re = acc_im = None
        for col in range(3):
            if dagger:
                link_re = links[direction, 0, col]
                link_im = links[direction, 1, col]
            else:
                link_re = links[direction, 0, :, col]
                link_im = links[direction, 1, :, col]
            re = half[0][slot][col][None]
            im = half[1][slot][col][None]
            if dagger:
                part_re = link_re * re + link_im * im
                part_im = link_re * im - link_im * re
            else:
                part_re = link_re * re - link_im * im
                part_im = link_re * im + link_im * re
            acc_re = part_re if acc_re is None else acc_re + part_re
            acc_im = part_im if acc_im is None else acc_im + part_im
        out[0][slot] = acc_re
        out[1][slot] = acc_im
    return out


def per_part(fn, half):
    return [[fn(half[part][slot]) for slot in range(2)] for part in range(2)]


def stack_half(half):
    return jnp.concatenate([half[p][s] for p in range(2) for s in range(2)], axis=0)


def split_half(stacked):
    return [[stacked[p * 6 + s * 3 : p * 6 + s * 3 + 3] for s in range(2)] for p in range(2)]


def split_bf16(value, pieces):
    out = []
    for _ in range(pieces):
        piece = value.astype(BF16)
        out.append(piece)
        value = value - piece.astype(F32)
    return out


def kernel(
    n_ta,
    n_gz,
    rows,
    source_hbm,
    links_hbm,
    clover_hbm,
    map_hbm,
    prolong_hbm,
    inverse_hbm,
    out_ref,
    source_in,
    links_in,
    clover_in,
    map_in,
    prolong_in,
    inverse,
    source,
    links,
    diag,
    recip,
    prolong,
    field,
    total,
    member,
    expander,
    projected,
    t_send,
    t_recv,
    z_send,
    z_recv,
    r_send,
    r_recv,
    c_send,
    c_recv,
    in_sem,
    halo_send_sem,
    halo_recv_sem,
    r_send_sem,
    r_recv_sem,
    c_send_sem,
    c_recv_sem,
):
    loads = [
        pltpu.make_async_copy(src, dst, in_sem.at[i])
        for i, (src, dst) in enumerate(
            (
                (source_hbm, source_in),
                (clover_hbm, clover_in),
                (links_hbm, links_in),
                (map_hbm, map_in),
                (prolong_hbm, prolong_in),
                (inverse_hbm, inverse),
            )
        )
    ]
    for load in loads:
        load.start()
    load_source, load_clover, load_links, load_map, load_prolong, load_inverse = loads

    ta = lax.axis_index("ta")
    gz = lax.axis_index("gz")
    t_before = lax.rem(ta + n_ta - 1, n_ta)
    t_after = lax.rem(ta + 1, n_ta)
    z_before = lax.rem(gz + n_gz - 1, n_gz)
    z_after = lax.rem(gz + 1, n_gz)
    peers = [lax.rem(gz + k, n_gz) for k in range(1, n_gz)]

    barrier = pltpu.get_barrier_semaphore()
    for there in (t_before, t_after):
        pl.semaphore_signal(barrier, inc=1, device_id=(there, gz), device_id_type=MESH)
    for there in peers:
        pl.semaphore_signal(barrier, inc=1, device_id=(ta, there), device_id_type=MESH)

    sub = lax.broadcasted_iota(jnp.int32, (8, HALF), 0)
    lane = lax.broadcasted_iota(jnp.int32, (8, HALF), 1)
    z_at = jnp.bitwise_and(sub, 3)
    x_at = jnp.bitwise_and(lane, LX - 1)

    def widen(dst, src, at, size):
        block = src[pl.ds(at, size)].astype(F32)
        dst[pl.ds(at, size), 0:4, :] = block[:, :, :HALF]
        dst[pl.ds(at, size), 4:8, :] = block[:, :, HALF:]

    load_source.wait()
    widen(source, source_in, 0, NCOMP)
    load_clover.wait()
    widen(diag, clover_in, 0, 12)
    for at in range(0, 12, 3):
        here = pl.ds(at, 3)
        wide = diag[here] + 3.6
        diag[here] = wide
        inv = 1.0 / wide
        recip[here] = inv
        for part in range(2):
            there = pl.ds(part * 12 + at, 3)
            field[there] = source[there] * inv

    pl.semaphore_wait(barrier, 2 + n_gz - 1)

    def select(mask, first, second):
        return jnp.where(mask[None], first, second)

    def shift(direction, step):
        def x_shift(value):
            if step > 0:
                return select(
                    x_at == LX - 1, pltpu.roll(value, LX - 1, 2), pltpu.roll(value, HALF - 1, 2)
                )
            return select(x_at == 0, pltpu.roll(value, HALF - LX + 1, 2), pltpu.roll(value, 1, 2))

        def y_shift(value):
            rolled = pltpu.roll(value, HALF - LX if step > 0 else LX, 2)
            swapped = pltpu.roll(rolled, 4, 1)
            return select(lane >= HALF - LX if step > 0 else lane < LX, swapped, rolled)

        return x_shift if direction == 0 else y_shift

    def pack_rows(stacked, row):
        blocks = []
        for block in range(3):
            packed = None
            for j in range(4):
                value = stacked[block * 4 + j]
                turn = (j - row) % 8
                if turn:
                    value = pltpu.roll(value, turn, 0)
                packed = value if packed is None else jnp.where(z_at == j, value, packed)
            blocks.append(packed)
        blocks.append(jnp.zeros((8, HALF), F32))
        return jnp.concatenate(blocks, axis=0).astype(BF16)

    def fill_rows(stacked, packed, row, turn):
        out = []
        for j in range(12):
            halo = packed[j // 4]
            by = (row - j % 4) % 8
            if by:
                halo = pltpu.roll(halo, by, 0)
            out.append(jnp.where(z_at == row, halo, pltpu.roll(stacked[j], turn, 0))[None])
        return jnp.concatenate(out, axis=0)

    def halo_copy(sweep, which, src, dst, device):
        return pltpu.make_async_remote_copy(
            src_ref=src,
            dst_ref=dst,
            send_sem=halo_send_sem.at[sweep, which],
            recv_sem=halo_recv_sem.at[sweep, which],
            device_id=device,
            device_id_type=MESH,
        )

    def hopping(sweep, before_links, beside):
        copies = [
            halo_copy(sweep, 0, t_send.at[sweep, 0], t_recv.at[sweep, 0], (t_before, gz)),
            halo_copy(sweep, 1, t_send.at[sweep, 1], t_recv.at[sweep, 1], (t_after, gz)),
            halo_copy(sweep, 2, z_send.at[sweep, 0], z_recv.at[sweep, 0], (ta, z_before)),
            halo_copy(sweep, 3, z_send.at[sweep, 1], z_recv.at[sweep, 1], (ta, z_after)),
        ]
        fwd_t = stack_half(project(field, 3, -1))
        t_send[sweep, 0] = fwd_t.reshape(96, HALF).astype(BF16)
        copies[0].start()
        fwd_z = stack_half(project(field, 2, -1))
        z_send[sweep, 0] = pack_rows(fwd_z, 0)
        copies[2].start()
        before_links()
        back_t = stack_half(mix(links, 3, project(field, 3, 1), True))
        t_send[sweep, 1] = back_t.reshape(96, HALF).astype(BF16)
        copies[1].start()
        back_z = stack_half(mix(links, 2, project(field, 2, 1), True))
        z_send[sweep, 1] = pack_rows(back_z, 3)
        copies[3].start()

        total[...] = jnp.zeros((NCOMP, 8, HALF), F32)
        for direction in range(2):
            ahead = per_part(shift(direction, 1), project(field, direction, -1))
            accumulate(total, mix(links, direction, ahead, False), direction, -1)
            behind = per_part(
                shift(direction, -1), mix(links, direction, project(field, direction, 1), True)
            )
            accumulate(total, behind, direction, 1)
        beside()
        for copy in copies:
            copy.wait()
        ahead_z = fill_rows(
            stack_half(project(field, 2, -1)),
            z_recv[sweep, 0].astype(F32).reshape(4, 8, HALF),
            3,
            7,
        )
        accumulate(total, mix(links, 2, split_half(ahead_z), False), 2, -1)
        behind_z = fill_rows(back_z, z_recv[sweep, 1].astype(F32).reshape(4, 8, HALF), 0, 1)
        accumulate(total, split_half(behind_z), 2, 1)
        ahead_t = t_recv[sweep, 0].astype(F32).reshape(12, 8, HALF)
        accumulate(total, mix(links, 3, split_half(ahead_t), False), 3, -1)
        behind_t = t_recv[sweep, 1].astype(F32).reshape(12, 8, HALF)
        accumulate(total, split_half(behind_t), 3, 1)

    def widen_links():
        load_links.wait()
        for direction in (3, 2, 1, 0):
            for part in range(2):
                for row in range(3):
                    at = direction * 18 + part * 9 + row * 3
                    block = links_in[pl.ds(at, 3)].astype(F32)
                    links[direction, part, row, :, 0:4, :] = block[:, :, :HALF]
                    links[direction, part, row, :, 4:8, :] = block[:, :, HALF:]

    def widen_prolong(start, stop):
        def step(i, carry):
            widen(prolong, prolong_in, i * 12, 12)
            return carry

        lax.fori_loop(start, stop, step, 0)

    def beside_first():
        load_map.wait()
        labels = lax.broadcasted_iota(jnp.int32, (NAGG, HALF), 0)
        ones = []
        for half in range(2):
            for z in range(4):
                row = map_in[pl.ds(z, 1), pl.ds(half * HALF, HALF)]
                ones.append((labels == row).astype(F32))
        member[...] = jnp.concatenate(ones, axis=0).astype(BF16)
        low = jnp.bitwise_and(
            lax.broadcasted_iota(jnp.int32, (HALF, NV * NAGG), 0), NAGG - 1
        ) * NV
        column = lax.broadcasted_iota(jnp.int32, (HALF, NV * NAGG), 1)
        inside = jnp.logical_and(column >= low, column < low + NV)
        expander[...] = inside.astype(F32).astype(BF16)
        load_prolong.wait()
        widen_prolong(0, 24)

    hopping(0, widen_links, beside_first)
    for at in range(0, 24, 3):
        here = pl.ds(at, 3)
        scale = pl.ds(at % 12, 3)
        first = field[here]
        resid = source[here] - diag[scale] * first + 0.5 * total[here]
        field[here] = first + resid * recip[scale]
    hopping(1, lambda: None, lambda: widen_prolong(24, 48))
    for at in range(0, 24, 3):
        here = pl.ds(at, 3)
        second = field[here]
        total[here] = source[here] - diag[pl.ds(at % 12, 3)] * second + 0.5 * total[here]

    def restrict(i, carry):
        accs = [None] * 4
        for comp in range(NCOMP):
            resid = total[comp]
            for k in range(4):
                term = prolong[(i * 4 + k) * NCOMP + comp] * resid
                accs[k] = term if accs[k] is None else accs[k] + term
        for k in range(4):
            projected[pl.ds((i * 4 + k) * 8, 8)] = accs[k]
        return carry

    lax.fori_loop(0, NV // 4, restrict, 0)

    member_value = member[...]
    sums = None
    for piece in split_bf16(projected[...], 3):
        term = lax.dot_general(
            piece, member_value, (((1,), (1,)), ((), ())), preferred_element_type=F32
        )
        sums = term if sums is None else sums + term
    own_group = (jnp.right_shift(lane, 5) == sub)[None]
    sums = jnp.sum(jnp.where(own_group, sums.reshape(NV, 8, HALF), 0.0), axis=1)
    spread_out = None
    expander_value = expander[...]
    for piece in split_bf16(sums, 3):
        term = jnp.dot(piece, expander_value, preferred_element_type=F32)
        spread_out = term if spread_out is None else spread_out + term
    column = lax.broadcasted_iota(jnp.int32, (NV, NV * NAGG), 1)
    vector = column - NV * jnp.right_shift(column * 2731, 16)
    at_vector = lax.broadcasted_iota(jnp.int32, (NV, NV * NAGG), 0) == vector
    r_send[...] = jnp.sum(jnp.where(at_vector, spread_out, 0.0), axis=0, keepdims=True)

    def to_peers(src, dst, send_sem, recv_sem):
        copies = [
            pltpu.make_async_remote_copy(
                src_ref=src,
                dst_ref=dst.at[k],
                send_sem=send_sem.at[k],
                recv_sem=recv_sem.at[k],
                device_id=(ta, there),
                device_id_type=MESH,
            )
            for k, there in enumerate(peers)
        ]
        for copy in copies:
            copy.start()
        return copies

    copies = to_peers(r_send, r_recv, r_send_sem, r_recv_sem)
    load_inverse.wait()
    for copy in copies:
        copy.wait()
    coarse = r_send[...]
    for k in range(n_gz - 1):
        coarse = coarse + r_recv[k]
    own_rows = jnp.sum(inverse[...] * coarse, axis=1, keepdims=True)
    label = jnp.bitwise_and(lax.broadcasted_iota(jnp.int32, (NV, 128), 1), NAGG - 1)
    owned = rows // NV
    placed = jnp.zeros((NV, 128), F32)
    for k in range(owned):
        placed = jnp.where(label == gz * owned + k, own_rows[k * NV : (k + 1) * NV], placed)
    c_send[...] = placed
    copies = to_peers(c_send, c_recv, c_send_sem, c_recv_sem)
    for copy in copies:
        copy.wait()
    correction = c_send[...]
    for k in range(n_gz - 1):
        correction = correction + c_recv[k]
    correction = jnp.concatenate([correction, correction], axis=1)
    lhs = jnp.where(own_group, jnp.broadcast_to(correction[:, None], (NV, 8, HALF)), 0.0)
    projected[...] = jnp.dot(
        lhs.reshape(NV * 8, HALF).astype(BF16), member_value, preferred_element_type=F32
    )

    def smooth(i, carry):
        accs = [field[i * 4 + k] for k in range(4)]
        for v in range(NV):
            weight = projected[pl.ds(v * 8, 8)]
            for k in range(4):
                accs[k] = accs[k] + prolong[v * NCOMP + i * 4 + k] * weight
        for k in range(4):
            out_ref[i * 4 + k, :, 0:HALF] = accs[k][0:4]
            out_ref[i * 4 + k, :, HALF : 2 * HALF] = accs[k][4:8]
        return carry

    lax.fori_loop(0, NCOMP // 4, smooth, 0)


def shards(n_ta, n_gz, source, links, clover, agg_map, prolong, inverse):
    rows = inverse.shape[1]
    vmem = pltpu.VMEM
    dma = pltpu.SemaphoreType.DMA
    out = pl.pallas_call(
        functools.partial(kernel, n_ta, n_gz, rows),
        out_shape=jax.ShapeDtypeStruct((24, 4, 512), F32),
        in_specs=[pl.BlockSpec(memory_space=pl.ANY)] * 6,
        out_specs=pl.BlockSpec(memory_space=pltpu.VMEM),
        scratch_shapes=[
            vmem((24, 4, 512), BF16),
            vmem((72, 4, 512), BF16),
            vmem((12, 4, 512), F32),
            vmem((4, 512), jnp.int32),
            vmem((576, 4, 512), BF16),
            vmem((rows, 768), F32),
            vmem((24, 8, HALF), F32),
            vmem((4, 2, 3, 3, 8, HALF), F32),
            vmem((12, 8, HALF), F32),
            vmem((12, 8, HALF), F32),
            vmem((576, 8, HALF), F32),
            vmem((24, 8, HALF), F32),
            vmem((24, 8, HALF), F32),
            vmem((256, HALF), BF16),
            vmem((256, 768), BF16),
            vmem((192, HALF), F32),
            vmem((2, 2, 96, HALF), BF16),
            vmem((2, 2, 96, HALF), BF16),
            vmem((2, 2, 32, HALF), BF16),
            vmem((2, 2, 32, HALF), BF16),
            vmem((1, 768), F32),
            vmem((n_gz - 1, 1, 768), F32),
            vmem((NV, 128), F32),
            vmem((n_gz - 1, NV, 128), F32),
            dma((6,)),
            dma((2, 4)),
            dma((2, 4)),
            dma((n_gz - 1,)),
            dma((n_gz - 1,)),
            dma((n_gz - 1,)),
            dma((n_gz - 1,)),
        ],
        compiler_params=pltpu.CompilerParams(
            collective_id=0, has_side_effects=True, vmem_limit_bytes=60 * 1024 * 1024
        ),
        cost_estimate=pl.CostEstimate(flops=20000000, bytes_accessed=4000000, transcendentals=0),
    )(
        source.reshape(24, 4, 512),
        links.reshape(72, 4, 512),
        clover.reshape(12, 4, 512),
        agg_map.reshape(4, 512),
        prolong.reshape(576, 4, 512),
        inverse.reshape(rows, 768),
    )
    return out.reshape(2, 4, 3, 1, 4, 512)


def solution(mesh):
    return jax.shard_map(
        functools.partial(shards, mesh.shape["ta"], mesh.shape["gz"]),
        mesh=mesh,
        in_specs=(
            P(None, None, None, "ta", "gz", None),
            P(None, None, None, None, "ta", "gz", None),
            P(None, None, "ta", "gz", None),
            P("ta", "gz", None),
            P(None, None, None, None, "ta", "gz", None),
            P("ta", "gz", None),
        ),
        out_specs=P(None, None, None, "ta", "gz", None),
        check_vma=False,
    )
```

```python
import functools

import jax
import jax.numpy as jnp
from jax import lax
from jax.experimental import pallas as pl
from jax.experimental.pallas import tpu as pltpu
from jax.sharding import PartitionSpec as P

LX = 32
NAGG = 32
NV = 24
NCOMP = 24
HALF = 256
GROUPS = 8

MESH = pl.DeviceIdType.MESH
F32 = jnp.float32
BF16 = jnp.bfloat16

spin_perms = ((3, 2, 1, 0), (3, 2, 1, 0), (2, 3, 0, 1), (2, 3, 0, 1))
spin_coefs = (
    ((1, -1), (1, -1), (1, 1), (1, 1)),
    ((0, -1), (0, 1), (0, 1), (0, -1)),
    ((1, -1), (1, 1), (1, 1), (1, -1)),
    ((0, 1), (0, 1), (0, 1), (0, 1)),
)


def add_signed(base, sign, value):
    return base + value if sign > 0 else base - value


def phase_terms(coef, sign):
    imag, coef_sign = coef
    total_sign = coef_sign * sign
    if imag:
        return (1, -total_sign), (0, total_sign)
    return (0, total_sign), (1, total_sign)


def project(field, direction, sign):
    parts = [[None, None], [None, None]]
    for slot in range(2):
        other = spin_perms[direction][slot]
        terms = phase_terms(spin_coefs[direction][slot], sign)
        for part in range(2):
            from_part, term_sign = terms[part]
            parts[part][slot] = add_signed(
                field[pl.ds(part * 12 + slot * 3, 3)],
                term_sign,
                field[pl.ds(from_part * 12 + other * 3, 3)],
            )
    return parts


def accumulate(total, half, direction, sign):
    for slot in range(2):
        other = spin_perms[direction][slot]
        terms = phase_terms(spin_coefs[direction][other], sign)
        for part in range(2):
            at = pl.ds(part * 12 + slot * 3, 3)
            total[at] = total[at] + half[part][slot]
            from_part, term_sign = terms[part]
            at = pl.ds(part * 12 + other * 3, 3)
            total[at] = add_signed(total[at], term_sign, half[from_part][slot])


def mix(links, direction, half, dagger):
    out = [[None, None], [None, None]]
    for slot in range(2):
        acc_re = acc_im = None
        for col in range(3):
            if dagger:
                link_re = links[direction, 0, col]
                link_im = links[direction, 1, col]
            else:
                link_re = links[direction, 0, :, col]
                link_im = links[direction, 1, :, col]
            re = half[0][slot][col][None]
            im = half[1][slot][col][None]
            if dagger:
                part_re = link_re * re + link_im * im
                part_im = link_re * im - link_im * re
            else:
                part_re = link_re * re - link_im * im
                part_im = link_re * im + link_im * re
            acc_re = part_re if acc_re is None else acc_re + part_re
            acc_im = part_im if acc_im is None else acc_im + part_im
        out[0][slot] = acc_re
        out[1][slot] = acc_im
    return out


def per_part(fn, half):
    return [[fn(half[part][slot]) for slot in range(2)] for part in range(2)]


def stack_half(half):
    return jnp.concatenate([half[p][s] for p in range(2) for s in range(2)], axis=0)


def split_half(stacked):
    return [[stacked[p * 6 + s * 3 : p * 6 + s * 3 + 3] for s in range(2)] for p in range(2)]


def split_bf16(value, pieces):
    out = []
    for _ in range(pieces):
        piece = value.astype(BF16)
        out.append(piece)
        value = value - piece.astype(F32)
    return out


def kernel(
    n_ta,
    n_gz,
    rows,
    source_hbm,
    links_hbm,
    clover_hbm,
    map_hbm,
    prolong_hbm,
    inverse_hbm,
    out_ref,
    source_in,
    links_in,
    clover_in,
    map_in,
    prolong_in,
    inverse,
    source,
    links,
    diag,
    recip,
    prolong,
    field,
    total,
    member,
    expander,
    projected,
    t_send,
    t_recv,
    z_send,
    z_recv,
    r_send,
    r_recv,
    c_send,
    c_recv,
    in_sem,
    halo_send_sem,
    halo_recv_sem,
    r_send_sem,
    r_recv_sem,
    c_send_sem,
    c_recv_sem,
):
    loads = [
        pltpu.make_async_copy(src, dst, in_sem.at[i])
        for i, (src, dst) in enumerate(
            (
                (source_hbm, source_in),
                (clover_hbm, clover_in),
                (links_hbm, links_in),
                (map_hbm, map_in),
                (prolong_hbm, prolong_in),
                (inverse_hbm, inverse),
            )
        )
    ]
    for load in loads:
        load.start()
    load_source, load_clover, load_links, load_map, load_prolong, load_inverse = loads

    ta = lax.axis_index("ta")
    gz = lax.axis_index("gz")
    t_before = lax.rem(ta + n_ta - 1, n_ta)
    t_after = lax.rem(ta + 1, n_ta)
    z_before = lax.rem(gz + n_gz - 1, n_gz)
    z_after = lax.rem(gz + 1, n_gz)
    peers = [lax.rem(gz + k, n_gz) for k in range(1, n_gz)]

    barrier = pltpu.get_barrier_semaphore()
    for there in (t_before, t_after):
        pl.semaphore_signal(barrier, inc=1, device_id=(there, gz), device_id_type=MESH)
    for there in peers:
        pl.semaphore_signal(barrier, inc=1, device_id=(ta, there), device_id_type=MESH)

    sub = lax.broadcasted_iota(jnp.int32, (8, HALF), 0)
    lane = lax.broadcasted_iota(jnp.int32, (8, HALF), 1)
    z_at = jnp.bitwise_and(sub, 3)
    x_at = jnp.bitwise_and(lane, LX - 1)

    def widen(dst, src, at, size):
        block = src[pl.ds(at, size)].astype(F32)
        dst[pl.ds(at, size), 0:4, :] = block[:, :, :HALF]
        dst[pl.ds(at, size), 4:8, :] = block[:, :, HALF:]

    load_source.wait()
    widen(source, source_in, 0, NCOMP)
    load_clover.wait()
    widen(diag, clover_in, 0, 12)
    for at in range(0, 12, 3):
        here = pl.ds(at, 3)
        wide = diag[here] + 3.6
        diag[here] = wide
        inv = 1.0 / wide
        recip[here] = inv
        for part in range(2):
            there = pl.ds(part * 12 + at, 3)
            field[there] = source[there] * inv

    def select(mask, first, second):
        return jnp.where(mask[None], first, second)

    def shift(direction, step):
        def x_shift(value):
            if step > 0:
                return select(
                    x_at == LX - 1, pltpu.roll(value, LX - 1, 2), pltpu.roll(value, HALF - 1, 2)
                )
            return select(x_at == 0, pltpu.roll(value, HALF - LX + 1, 2), pltpu.roll(value, 1, 2))

        def y_shift(value):
            rolled = pltpu.roll(value, HALF - LX if step > 0 else LX, 2)
            swapped = pltpu.roll(rolled, 4, 1)
            return select(lane >= HALF - LX if step > 0 else lane < LX, swapped, rolled)

        return x_shift if direction == 0 else y_shift

    def pack_rows(stacked, row):
        blocks = []
        for block in range(3):
            packed = None
            for j in range(4):
                value = stacked[block * 4 + j]
                turn = (j - row) % 8
                if turn:
                    value = pltpu.roll(value, turn, 0)
                packed = value if packed is None else jnp.where(z_at == j, value, packed)
            blocks.append(packed)
        blocks.append(jnp.zeros((8, HALF), F32))
        return jnp.concatenate(blocks, axis=0).astype(BF16)

    def fill_rows(stacked, packed, row, turn):
        out = []
        for j in range(12):
            halo = packed[j // 4]
            by = (row - j % 4) % 8
            if by:
                halo = pltpu.roll(halo, by, 0)
            out.append(jnp.where(z_at == row, halo, pltpu.roll(stacked[j], turn, 0))[None])
        return jnp.concatenate(out, axis=0)

    def halo_copy(sweep, which, src, dst, device):
        return pltpu.make_async_remote_copy(
            src_ref=src,
            dst_ref=dst,
            send_sem=halo_send_sem.at[sweep, which],
            recv_sem=halo_recv_sem.at[sweep, which],
            device_id=device,
            device_id_type=MESH,
        )

    def hopping(sweep, before_links, beside):
        copies = [
            halo_copy(sweep, 0, t_send.at[sweep, 0], t_recv.at[sweep, 0], (t_before, gz)),
            halo_copy(sweep, 1, t_send.at[sweep, 1], t_recv.at[sweep, 1], (t_after, gz)),
            halo_copy(sweep, 2, z_send.at[sweep, 0], z_recv.at[sweep, 0], (ta, z_before)),
            halo_copy(sweep, 3, z_send.at[sweep, 1], z_recv.at[sweep, 1], (ta, z_after)),
        ]
        fwd_t = stack_half(project(field, 3, -1))
        t_send[sweep, 0] = fwd_t.reshape(96, HALF).astype(BF16)
        if sweep == 1:
            copies[0].start()
        fwd_z = stack_half(project(field, 2, -1))
        z_send[sweep, 0] = pack_rows(fwd_z, 0)
        if sweep == 1:
            copies[2].start()
        before_links()
        back_t = stack_half(mix(links, 3, project(field, 3, 1), True))
        t_send[sweep, 1] = back_t.reshape(96, HALF).astype(BF16)
        if sweep == 1:
            copies[1].start()
        back_z = stack_half(mix(links, 2, project(field, 2, 1), True))
        z_send[sweep, 1] = pack_rows(back_z, 3)
        if sweep == 1:
            copies[3].start()

        if sweep == 0:
            beside()
            pl.semaphore_wait(barrier, 2 + n_gz - 1)
            for which in (1, 0, 3, 2):
                copies[which].start()

        total[...] = jnp.zeros((NCOMP, 8, HALF), F32)
        for direction in range(2):
            ahead = per_part(shift(direction, 1), project(field, direction, -1))
            accumulate(total, mix(links, direction, ahead, False), direction, -1)
            behind = per_part(
                shift(direction, -1), mix(links, direction, project(field, direction, 1), True)
            )
            accumulate(total, behind, direction, 1)
        if sweep == 1:
            beside()
        for copy in copies:
            copy.wait()
        ahead_z = fill_rows(
            stack_half(project(field, 2, -1)),
            z_recv[sweep, 0].astype(F32).reshape(4, 8, HALF),
            3,
            7,
        )
        accumulate(total, mix(links, 2, split_half(ahead_z), False), 2, -1)
        behind_z = fill_rows(back_z, z_recv[sweep, 1].astype(F32).reshape(4, 8, HALF), 0, 1)
        accumulate(total, split_half(behind_z), 2, 1)
        ahead_t = t_recv[sweep, 0].astype(F32).reshape(12, 8, HALF)
        accumulate(total, mix(links, 3, split_half(ahead_t), False), 3, -1)
        behind_t = t_recv[sweep, 1].astype(F32).reshape(12, 8, HALF)
        accumulate(total, split_half(behind_t), 3, 1)

    def widen_links():
        load_links.wait()
        for direction in (3, 2, 1, 0):
            for part in range(2):
                for row in range(3):
                    at = direction * 18 + part * 9 + row * 3
                    block = links_in[pl.ds(at, 3)].astype(F32)
                    links[direction, part, row, :, 0:4, :] = block[:, :, :HALF]
                    links[direction, part, row, :, 4:8, :] = block[:, :, HALF:]

    def widen_prolong(start, stop):
        def step(i, carry):
            widen(prolong, prolong_in, i * 12, 12)
            return carry

        lax.fori_loop(start, stop, step, 0)

    def beside_first():
        load_map.wait()
        labels = lax.broadcasted_iota(jnp.int32, (NAGG, HALF), 0)
        ones = []
        for half in range(2):
            for z in range(4):
                row = map_in[pl.ds(z, 1), pl.ds(half * HALF, HALF)]
                ones.append((labels == row).astype(F32))
        member[...] = jnp.concatenate(ones, axis=0).astype(BF16)
        low = jnp.bitwise_and(
            lax.broadcasted_iota(jnp.int32, (HALF, NV * NAGG), 0), NAGG - 1
        ) * NV
        column = lax.broadcasted_iota(jnp.int32, (HALF, NV * NAGG), 1)
        inside = jnp.logical_and(column >= low, column < low + NV)
        expander[...] = inside.astype(F32).astype(BF16)
        load_prolong.wait()
        widen_prolong(0, 24)

    hopping(0, widen_links, beside_first)
    for at in range(0, 24, 3):
        here = pl.ds(at, 3)
        scale = pl.ds(at % 12, 3)
        first = field[here]
        resid = source[here] - diag[scale] * first + 0.5 * total[here]
        field[here] = first + resid * recip[scale]
    hopping(1, lambda: None, lambda: widen_prolong(24, 48))
    for at in range(0, 24, 3):
        here = pl.ds(at, 3)
        second = field[here]
        total[here] = source[here] - diag[pl.ds(at % 12, 3)] * second + 0.5 * total[here]

    def restrict(i, carry):
        accs = [None] * 4
        for comp in range(NCOMP):
            resid = total[comp]
            for k in range(4):
                term = prolong[(i * 4 + k) * NCOMP + comp] * resid
                accs[k] = term if accs[k] is None else accs[k] + term
        for k in range(4):
            projected[pl.ds((i * 4 + k) * 8, 8)] = accs[k]
        return carry

    lax.fori_loop(0, NV // 4, restrict, 0)

    member_value = member[...]
    sums = None
    for piece in split_bf16(projected[...], 3):
        term = lax.dot_general(
            piece, member_value, (((1,), (1,)), ((), ())), preferred_element_type=F32
        )
        sums = term if sums is None else sums + term
    own_group = (jnp.right_shift(lane, 5) == sub)[None]
    sums = jnp.sum(jnp.where(own_group, sums.reshape(NV, 8, HALF), 0.0), axis=1)
    spread_out = None
    expander_value = expander[...]
    for piece in split_bf16(sums, 3):
        term = jnp.dot(piece, expander_value, preferred_element_type=F32)
        spread_out = term if spread_out is None else spread_out + term
    column = lax.broadcasted_iota(jnp.int32, (NV, NV * NAGG), 1)
    vector = column - NV * jnp.right_shift(column * 2731, 16)
    at_vector = lax.broadcasted_iota(jnp.int32, (NV, NV * NAGG), 0) == vector
    r_send[...] = jnp.sum(jnp.where(at_vector, spread_out, 0.0), axis=0, keepdims=True)

    def to_peers(src, dst, send_sem, recv_sem):
        copies = [
            pltpu.make_async_remote_copy(
                src_ref=src,
                dst_ref=dst.at[k],
                send_sem=send_sem.at[k],
                recv_sem=recv_sem.at[k],
                device_id=(ta, there),
                device_id_type=MESH,
            )
            for k, there in enumerate(peers)
        ]
        for copy in copies:
            copy.start()
        return copies

    copies = to_peers(r_send, r_recv, r_send_sem, r_recv_sem)
    load_inverse.wait()
    for copy in copies:
        copy.wait()
    coarse = r_send[...]
    for k in range(n_gz - 1):
        coarse = coarse + r_recv[k]
    own_rows = jnp.sum(inverse[...] * coarse, axis=1, keepdims=True)
    label = jnp.bitwise_and(lax.broadcasted_iota(jnp.int32, (NV, 128), 1), NAGG - 1)
    owned = rows // NV
    placed = jnp.zeros((NV, 128), F32)
    for k in range(owned):
        placed = jnp.where(label == gz * owned + k, own_rows[k * NV : (k + 1) * NV], placed)
    c_send[...] = placed
    copies = to_peers(c_send, c_recv, c_send_sem, c_recv_sem)
    for copy in copies:
        copy.wait()
    correction = c_send[...]
    for k in range(n_gz - 1):
        correction = correction + c_recv[k]
    correction = jnp.concatenate([correction, correction], axis=1)
    lhs = jnp.where(own_group, jnp.broadcast_to(correction[:, None], (NV, 8, HALF)), 0.0)
    projected[...] = jnp.dot(
        lhs.reshape(NV * 8, HALF).astype(BF16), member_value, preferred_element_type=F32
    )

    def smooth(i, carry):
        accs = [field[i * 4 + k] for k in range(4)]
        for v in range(NV):
            weight = projected[pl.ds(v * 8, 8)]
            for k in range(4):
                accs[k] = accs[k] + prolong[v * NCOMP + i * 4 + k] * weight
        for k in range(4):
            out_ref[i * 4 + k, :, 0:HALF] = accs[k][0:4]
            out_ref[i * 4 + k, :, HALF : 2 * HALF] = accs[k][4:8]
        return carry

    lax.fori_loop(0, NCOMP // 4, smooth, 0)


def shards(n_ta, n_gz, source, links, clover, agg_map, prolong, inverse):
    rows = inverse.shape[1]
    vmem = pltpu.VMEM
    dma = pltpu.SemaphoreType.DMA
    out = pl.pallas_call(
        functools.partial(kernel, n_ta, n_gz, rows),
        out_shape=jax.ShapeDtypeStruct((24, 4, 512), F32),
        in_specs=[pl.BlockSpec(memory_space=pl.ANY)] * 6,
        out_specs=pl.BlockSpec(memory_space=pltpu.VMEM),
        scratch_shapes=[
            vmem((24, 4, 512), BF16),
            vmem((72, 4, 512), BF16),
            vmem((12, 4, 512), F32),
            vmem((4, 512), jnp.int32),
            vmem((576, 4, 512), BF16),
            vmem((rows, 768), F32),
            vmem((24, 8, HALF), F32),
            vmem((4, 2, 3, 3, 8, HALF), F32),
            vmem((12, 8, HALF), F32),
            vmem((12, 8, HALF), F32),
            vmem((576, 8, HALF), F32),
            vmem((24, 8, HALF), F32),
            vmem((24, 8, HALF), F32),
            vmem((256, HALF), BF16),
            vmem((256, 768), BF16),
            vmem((192, HALF), F32),
            vmem((2, 2, 96, HALF), BF16),
            vmem((2, 2, 96, HALF), BF16),
            vmem((2, 2, 32, HALF), BF16),
            vmem((2, 2, 32, HALF), BF16),
            vmem((1, 768), F32),
            vmem((n_gz - 1, 1, 768), F32),
            vmem((NV, 128), F32),
            vmem((n_gz - 1, NV, 128), F32),
            dma((6,)),
            dma((2, 4)),
            dma((2, 4)),
            dma((n_gz - 1,)),
            dma((n_gz - 1,)),
            dma((n_gz - 1,)),
            dma((n_gz - 1,)),
        ],
        compiler_params=pltpu.CompilerParams(
            collective_id=0, has_side_effects=True, vmem_limit_bytes=60 * 1024 * 1024
        ),
        cost_estimate=pl.CostEstimate(flops=20000000, bytes_accessed=4000000, transcendentals=0),
    )(
        source.reshape(24, 4, 512),
        links.reshape(72, 4, 512),
        clover.reshape(12, 4, 512),
        agg_map.reshape(4, 512),
        prolong.reshape(576, 4, 512),
        inverse.reshape(rows, 768),
    )
    return out.reshape(2, 4, 3, 1, 4, 512)


def solution(mesh):
    return jax.shard_map(
        functools.partial(shards, mesh.shape["ta"], mesh.shape["gz"]),
        mesh=mesh,
        in_specs=(
            P(None, None, None, "ta", "gz", None),
            P(None, None, None, None, "ta", "gz", None),
            P(None, None, "ta", "gz", None),
            P("ta", "gz", None),
            P(None, None, None, None, "ta", "gz", None),
            P("ta", "gz", None),
        ),
        out_specs=P(None, None, None, "ta", "gz", None),
        check_vma=False,
    )
```

```python
import functools

import jax
import jax.numpy as jnp
from jax import lax
from jax.experimental import pallas as pl
from jax.experimental.pallas import tpu as pltpu
from jax.sharding import PartitionSpec as P

LX = 32
NAGG = 32
NV = 24
NCOMP = 24
HALF = 256
GROUPS = 8

MESH = pl.DeviceIdType.MESH
F32 = jnp.float32
BF16 = jnp.bfloat16

spin_perms = ((3, 2, 1, 0), (3, 2, 1, 0), (2, 3, 0, 1), (2, 3, 0, 1))
spin_coefs = (
    ((1, -1), (1, -1), (1, 1), (1, 1)),
    ((0, -1), (0, 1), (0, 1), (0, -1)),
    ((1, -1), (1, 1), (1, 1), (1, -1)),
    ((0, 1), (0, 1), (0, 1), (0, 1)),
)


def add_signed(base, sign, value):
    return base + value if sign > 0 else base - value


def phase_terms(coef, sign):
    imag, coef_sign = coef
    total_sign = coef_sign * sign
    if imag:
        return (1, -total_sign), (0, total_sign)
    return (0, total_sign), (1, total_sign)


def project(field, direction, sign):
    parts = [[None, None], [None, None]]
    for slot in range(2):
        other = spin_perms[direction][slot]
        terms = phase_terms(spin_coefs[direction][slot], sign)
        for part in range(2):
            from_part, term_sign = terms[part]
            parts[part][slot] = add_signed(
                field[pl.ds(part * 12 + slot * 3, 3)],
                term_sign,
                field[pl.ds(from_part * 12 + other * 3, 3)],
            )
    return parts


def accumulate(total, half, direction, sign):
    for slot in range(2):
        other = spin_perms[direction][slot]
        terms = phase_terms(spin_coefs[direction][other], sign)
        for part in range(2):
            at = pl.ds(part * 12 + slot * 3, 3)
            total[at] = total[at] + half[part][slot]
            from_part, term_sign = terms[part]
            at = pl.ds(part * 12 + other * 3, 3)
            total[at] = add_signed(total[at], term_sign, half[from_part][slot])


def mix(links, direction, half, dagger):
    out = [[None, None], [None, None]]
    for slot in range(2):
        acc_re = acc_im = None
        for col in range(3):
            if dagger:
                link_re = links[direction, 0, col]
                link_im = links[direction, 1, col]
            else:
                link_re = links[direction, 0, :, col]
                link_im = links[direction, 1, :, col]
            re = half[0][slot][col][None]
            im = half[1][slot][col][None]
            if dagger:
                part_re = link_re * re + link_im * im
                part_im = link_re * im - link_im * re
            else:
                part_re = link_re * re - link_im * im
                part_im = link_re * im + link_im * re
            acc_re = part_re if acc_re is None else acc_re + part_re
            acc_im = part_im if acc_im is None else acc_im + part_im
        out[0][slot] = acc_re
        out[1][slot] = acc_im
    return out


def per_part(fn, half):
    return [[fn(half[part][slot]) for slot in range(2)] for part in range(2)]


def stack_half(half):
    return jnp.concatenate([half[p][s] for p in range(2) for s in range(2)], axis=0)


def split_half(stacked):
    return [[stacked[p * 6 + s * 3 : p * 6 + s * 3 + 3] for s in range(2)] for p in range(2)]


def split_bf16(value, pieces):
    out = []
    for _ in range(pieces):
        piece = value.astype(BF16)
        out.append(piece)
        value = value - piece.astype(F32)
    return out


def kernel(
    n_ta,
    n_gz,
    rows,
    source_hbm,
    links_hbm,
    clover_hbm,
    map_hbm,
    prolong_hbm,
    inverse_hbm,
    out_ref,
    source_in,
    links_in,
    clover_in,
    map_in,
    prolong_in,
    inverse,
    source,
    links,
    diag,
    recip,
    prolong,
    field,
    total,
    member,
    expander,
    projected,
    t_send,
    t_recv,
    z_send,
    z_recv,
    r_send,
    r_recv,
    c_send,
    c_recv,
    in_sem,
    halo_send_sem,
    halo_recv_sem,
    r_send_sem,
    r_recv_sem,
    c_send_sem,
    c_recv_sem,
):
    loads = [
        pltpu.make_async_copy(src, dst, in_sem.at[i])
        for i, (src, dst) in enumerate(
            (
                (source_hbm, source_in),
                (clover_hbm, clover_in),
                (links_hbm, links_in),
                (map_hbm, map_in),
                (prolong_hbm, prolong_in),
                (inverse_hbm, inverse),
            )
        )
    ]
    for load in loads[:4]:
        load.start()
    load_source, load_clover, load_links, load_map, load_prolong, load_inverse = loads

    ta = lax.axis_index("ta")
    gz = lax.axis_index("gz")
    t_before = lax.rem(ta + n_ta - 1, n_ta)
    t_after = lax.rem(ta + 1, n_ta)
    z_before = lax.rem(gz + n_gz - 1, n_gz)
    z_after = lax.rem(gz + 1, n_gz)
    peers = [lax.rem(gz + k, n_gz) for k in range(1, n_gz)]

    barrier = pltpu.get_barrier_semaphore()
    for there in (t_before, t_after):
        pl.semaphore_signal(barrier, inc=1, device_id=(there, gz), device_id_type=MESH)
    for there in peers:
        pl.semaphore_signal(barrier, inc=1, device_id=(ta, there), device_id_type=MESH)

    sub = lax.broadcasted_iota(jnp.int32, (8, HALF), 0)
    lane = lax.broadcasted_iota(jnp.int32, (8, HALF), 1)
    z_at = jnp.bitwise_and(sub, 3)
    x_at = jnp.bitwise_and(lane, LX - 1)

    def widen(dst, src, at, size):
        block = src[pl.ds(at, size)].astype(F32)
        dst[pl.ds(at, size), 0:4, :] = block[:, :, :HALF]
        dst[pl.ds(at, size), 4:8, :] = block[:, :, HALF:]

    load_source.wait()
    widen(source, source_in, 0, NCOMP)
    load_clover.wait()
    widen(diag, clover_in, 0, 12)
    for at in range(0, 12, 3):
        here = pl.ds(at, 3)
        wide = diag[here] + 3.6
        diag[here] = wide
        inv = 1.0 / wide
        recip[here] = inv
        for part in range(2):
            there = pl.ds(part * 12 + at, 3)
            field[there] = source[there] * inv

    pl.semaphore_wait(barrier, 2 + n_gz - 1)

    def select(mask, first, second):
        return jnp.where(mask[None], first, second)

    def shift(direction, step):
        def x_shift(value):
            if step > 0:
                return select(
                    x_at == LX - 1, pltpu.roll(value, LX - 1, 2), pltpu.roll(value, HALF - 1, 2)
                )
            return select(x_at == 0, pltpu.roll(value, HALF - LX + 1, 2), pltpu.roll(value, 1, 2))

        def y_shift(value):
            rolled = pltpu.roll(value, HALF - LX if step > 0 else LX, 2)
            swapped = pltpu.roll(rolled, 4, 1)
            return select(lane >= HALF - LX if step > 0 else lane < LX, swapped, rolled)

        return x_shift if direction == 0 else y_shift

    def pack_rows(stacked, row):
        blocks = []
        for block in range(3):
            packed = None
            for j in range(4):
                value = stacked[block * 4 + j]
                turn = (j - row) % 8
                if turn:
                    value = pltpu.roll(value, turn, 0)
                packed = value if packed is None else jnp.where(z_at == j, value, packed)
            blocks.append(packed)
        blocks.append(jnp.zeros((8, HALF), F32))
        return jnp.concatenate(blocks, axis=0).astype(BF16)

    def fill_rows(stacked, packed, row, turn):
        out = []
        for j in range(12):
            halo = packed[j // 4]
            by = (row - j % 4) % 8
            if by:
                halo = pltpu.roll(halo, by, 0)
            out.append(jnp.where(z_at == row, halo, pltpu.roll(stacked[j], turn, 0))[None])
        return jnp.concatenate(out, axis=0)

    def halo_copy(sweep, which, src, dst, device):
        return pltpu.make_async_remote_copy(
            src_ref=src,
            dst_ref=dst,
            send_sem=halo_send_sem.at[sweep, which],
            recv_sem=halo_recv_sem.at[sweep, which],
            device_id=device,
            device_id_type=MESH,
        )

    def hopping(sweep, before_links, beside):
        copies = [
            halo_copy(sweep, 0, t_send.at[sweep, 0], t_recv.at[sweep, 0], (t_before, gz)),
            halo_copy(sweep, 1, t_send.at[sweep, 1], t_recv.at[sweep, 1], (t_after, gz)),
            halo_copy(sweep, 2, z_send.at[sweep, 0], z_recv.at[sweep, 0], (ta, z_before)),
            halo_copy(sweep, 3, z_send.at[sweep, 1], z_recv.at[sweep, 1], (ta, z_after)),
        ]
        fwd_t = stack_half(project(field, 3, -1))
        t_send[sweep, 0] = fwd_t.reshape(96, HALF).astype(BF16)
        copies[0].start()
        fwd_z = stack_half(project(field, 2, -1))
        z_send[sweep, 0] = pack_rows(fwd_z, 0)
        copies[2].start()
        before_links()
        back_t = stack_half(mix(links, 3, project(field, 3, 1), True))
        t_send[sweep, 1] = back_t.reshape(96, HALF).astype(BF16)
        copies[1].start()
        back_z = stack_half(mix(links, 2, project(field, 2, 1), True))
        z_send[sweep, 1] = pack_rows(back_z, 3)
        copies[3].start()

        total[...] = jnp.zeros((NCOMP, 8, HALF), F32)
        for direction in range(2):
            ahead = per_part(shift(direction, 1), project(field, direction, -1))
            accumulate(total, mix(links, direction, ahead, False), direction, -1)
            behind = per_part(
                shift(direction, -1), mix(links, direction, project(field, direction, 1), True)
            )
            accumulate(total, behind, direction, 1)
        beside()
        for copy in copies:
            copy.wait()
        ahead_z = fill_rows(
            stack_half(project(field, 2, -1)),
            z_recv[sweep, 0].astype(F32).reshape(4, 8, HALF),
            3,
            7,
        )
        accumulate(total, mix(links, 2, split_half(ahead_z), False), 2, -1)
        behind_z = fill_rows(back_z, z_recv[sweep, 1].astype(F32).reshape(4, 8, HALF), 0, 1)
        accumulate(total, split_half(behind_z), 2, 1)
        ahead_t = t_recv[sweep, 0].astype(F32).reshape(12, 8, HALF)
        accumulate(total, mix(links, 3, split_half(ahead_t), False), 3, -1)
        behind_t = t_recv[sweep, 1].astype(F32).reshape(12, 8, HALF)
        accumulate(total, split_half(behind_t), 3, 1)

    def widen_links():
        load_links.wait()
        load_prolong.start()
        load_inverse.start()
        for direction in (3, 2, 1, 0):
            for part in range(2):
                for row in range(3):
                    at = direction * 18 + part * 9 + row * 3
                    block = links_in[pl.ds(at, 3)].astype(F32)
                    links[direction, part, row, :, 0:4, :] = block[:, :, :HALF]
                    links[direction, part, row, :, 4:8, :] = block[:, :, HALF:]

    def widen_prolong(start, stop):
        def step(i, carry):
            widen(prolong, prolong_in, i * 12, 12)
            return carry

        lax.fori_loop(start, stop, step, 0)

    def beside_first():
        load_map.wait()
        labels = lax.broadcasted_iota(jnp.int32, (NAGG, HALF), 0)
        ones = []
        for half in range(2):
            for z in range(4):
                row = map_in[pl.ds(z, 1), pl.ds(half * HALF, HALF)]
                ones.append((labels == row).astype(F32))
        member[...] = jnp.concatenate(ones, axis=0).astype(BF16)
        low = jnp.bitwise_and(
            lax.broadcasted_iota(jnp.int32, (HALF, NV * NAGG), 0), NAGG - 1
        ) * NV
        column = lax.broadcasted_iota(jnp.int32, (HALF, NV * NAGG), 1)
        inside = jnp.logical_and(column >= low, column < low + NV)
        expander[...] = inside.astype(F32).astype(BF16)
        load_prolong.wait()
        widen_prolong(0, 24)

    hopping(0, widen_links, beside_first)
    for at in range(0, 24, 3):
        here = pl.ds(at, 3)
        scale = pl.ds(at % 12, 3)
        first = field[here]
        resid = source[here] - diag[scale] * first + 0.5 * total[here]
        field[here] = first + resid * recip[scale]
    hopping(1, lambda: None, lambda: widen_prolong(24, 48))
    for at in range(0, 24, 3):
        here = pl.ds(at, 3)
        second = field[here]
        total[here] = source[here] - diag[pl.ds(at % 12, 3)] * second + 0.5 * total[here]

    def restrict(i, carry):
        accs = [None] * 4
        for comp in range(NCOMP):
            resid = total[comp]
            for k in range(4):
                term = prolong[(i * 4 + k) * NCOMP + comp] * resid
                accs[k] = term if accs[k] is None else accs[k] + term
        for k in range(4):
            projected[pl.ds((i * 4 + k) * 8, 8)] = accs[k]
        return carry

    lax.fori_loop(0, NV // 4, restrict, 0)

    member_value = member[...]
    sums = None
    for piece in split_bf16(projected[...], 3):
        term = lax.dot_general(
            piece, member_value, (((1,), (1,)), ((), ())), preferred_element_type=F32
        )
        sums = term if sums is None else sums + term
    own_group = (jnp.right_shift(lane, 5) == sub)[None]
    sums = jnp.sum(jnp.where(own_group, sums.reshape(NV, 8, HALF), 0.0), axis=1)
    spread_out = None
    expander_value = expander[...]
    for piece in split_bf16(sums, 3):
        term = jnp.dot(piece, expander_value, preferred_element_type=F32)
        spread_out = term if spread_out is None else spread_out + term
    column = lax.broadcasted_iota(jnp.int32, (NV, NV * NAGG), 1)
    vector = column - NV * jnp.right_shift(column * 2731, 16)
    at_vector = lax.broadcasted_iota(jnp.int32, (NV, NV * NAGG), 0) == vector
    r_send[...] = jnp.sum(jnp.where(at_vector, spread_out, 0.0), axis=0, keepdims=True)

    def to_peers(src, dst, send_sem, recv_sem):
        copies = [
            pltpu.make_async_remote_copy(
                src_ref=src,
                dst_ref=dst.at[k],
                send_sem=send_sem.at[k],
                recv_sem=recv_sem.at[k],
                device_id=(ta, there),
                device_id_type=MESH,
            )
            for k, there in enumerate(peers)
        ]
        for copy in copies:
            copy.start()
        return copies

    copies = to_peers(r_send, r_recv, r_send_sem, r_recv_sem)
    load_inverse.wait()
    for copy in copies:
        copy.wait()
    coarse = r_send[...]
    for k in range(n_gz - 1):
        coarse = coarse + r_recv[k]
    own_rows = jnp.sum(inverse[...] * coarse, axis=1, keepdims=True)
    label = jnp.bitwise_and(lax.broadcasted_iota(jnp.int32, (NV, 128), 1), NAGG - 1)
    owned = rows // NV
    placed = jnp.zeros((NV, 128), F32)
    for k in range(owned):
        placed = jnp.where(label == gz * owned + k, own_rows[k * NV : (k + 1) * NV], placed)
    c_send[...] = placed
    copies = to_peers(c_send, c_recv, c_send_sem, c_recv_sem)
    for copy in copies:
        copy.wait()
    correction = c_send[...]
    for k in range(n_gz - 1):
        correction = correction + c_recv[k]
    correction = jnp.concatenate([correction, correction], axis=1)
    lhs = jnp.where(own_group, jnp.broadcast_to(correction[:, None], (NV, 8, HALF)), 0.0)
    projected[...] = jnp.dot(
        lhs.reshape(NV * 8, HALF).astype(BF16), member_value, preferred_element_type=F32
    )

    def smooth(i, carry):
        accs = [field[i * 4 + k] for k in range(4)]
        for v in range(NV):
            weight = projected[pl.ds(v * 8, 8)]
            for k in range(4):
                accs[k] = accs[k] + prolong[v * NCOMP + i * 4 + k] * weight
        for k in range(4):
            out_ref[i * 4 + k, :, 0:HALF] = accs[k][0:4]
            out_ref[i * 4 + k, :, HALF : 2 * HALF] = accs[k][4:8]
        return carry

    lax.fori_loop(0, NCOMP // 4, smooth, 0)


def shards(n_ta, n_gz, source, links, clover, agg_map, prolong, inverse):
    rows = inverse.shape[1]
    vmem = pltpu.VMEM
    dma = pltpu.SemaphoreType.DMA
    out = pl.pallas_call(
        functools.partial(kernel, n_ta, n_gz, rows),
        out_shape=jax.ShapeDtypeStruct((24, 4, 512), F32),
        in_specs=[pl.BlockSpec(memory_space=pl.ANY)] * 6,
        out_specs=pl.BlockSpec(memory_space=pltpu.VMEM),
        scratch_shapes=[
            vmem((24, 4, 512), BF16),
            vmem((72, 4, 512), BF16),
            vmem((12, 4, 512), F32),
            vmem((4, 512), jnp.int32),
            vmem((576, 4, 512), BF16),
            vmem((rows, 768), F32),
            vmem((24, 8, HALF), F32),
            vmem((4, 2, 3, 3, 8, HALF), F32),
            vmem((12, 8, HALF), F32),
            vmem((12, 8, HALF), F32),
            vmem((576, 8, HALF), F32),
            vmem((24, 8, HALF), F32),
            vmem((24, 8, HALF), F32),
            vmem((256, HALF), BF16),
            vmem((256, 768), BF16),
            vmem((192, HALF), F32),
            vmem((2, 2, 96, HALF), BF16),
            vmem((2, 2, 96, HALF), BF16),
            vmem((2, 2, 32, HALF), BF16),
            vmem((2, 2, 32, HALF), BF16),
            vmem((1, 768), F32),
            vmem((n_gz - 1, 1, 768), F32),
            vmem((NV, 128), F32),
            vmem((n_gz - 1, NV, 128), F32),
            dma((6,)),
            dma((2, 4)),
            dma((2, 4)),
            dma((n_gz - 1,)),
            dma((n_gz - 1,)),
            dma((n_gz - 1,)),
            dma((n_gz - 1,)),
        ],
        compiler_params=pltpu.CompilerParams(
            collective_id=0, has_side_effects=True, vmem_limit_bytes=60 * 1024 * 1024
        ),
        cost_estimate=pl.CostEstimate(flops=20000000, bytes_accessed=4000000, transcendentals=0),
    )(
        source.reshape(24, 4, 512),
        links.reshape(72, 4, 512),
        clover.reshape(12, 4, 512),
        agg_map.reshape(4, 512),
        prolong.reshape(576, 4, 512),
        inverse.reshape(rows, 768),
    )
    return out.reshape(2, 4, 3, 1, 4, 512)


def solution(mesh):
    return jax.shard_map(
        functools.partial(shards, mesh.shape["ta"], mesh.shape["gz"]),
        mesh=mesh,
        in_specs=(
            P(None, None, None, "ta", "gz", None),
            P(None, None, None, None, "ta", "gz", None),
            P(None, None, "ta", "gz", None),
            P("ta", "gz", None),
            P(None, None, None, None, "ta", "gz", None),
            P("ta", "gz", None),
        ),
        out_specs=P(None, None, None, "ta", "gz", None),
        check_vma=False,
    )
```
